32 devices in a mesh: shard: 4 (over y, x), example: 8 (over z, core).
Axes of the slice: x: 2, y: 2, z: 4, core: 2. Of those that a mesh axis runs over, the one named last changes fastest.
Arguments:
- activations: bfloat16 [768, 128, 4096], P('example', None, 'shard'), may hold values from -6 to 6
- out_grads: bfloat16 [768, 128, 4096], P('example', None, 'shard'), may hold values from -6 to 6
- lengths: int32 [768], P('example'), may hold values from 1 to 128
- proj_in: bfloat16 [128, 4096], P(None, 'shard'), may hold values from -0.09375 to 0.09375
- proj_out: bfloat16 [64, 4096], P(None, 'shard'), may hold values from -0.09375 to 0.09375
Outputs:
- ntk_kernel: float32 [768, 768], P('example', 'shard')
The draws below stay inside these ranges and needn't reach their ends.
All inputs are finite; a program needn't handle non-finite values.
Results may differ from the reference program's by a relative error of at most 0.0014.
Values may be sent and summed in bfloat16 or wider, within the bound.
A program may use at most 128 MiB of HBM per device.

```python
import math
import jax
import jax.numpy as jnp
from jax import lax

D = 4096
R_OUT = 64
R_IN = 128
LEN = 128
SEQS = 768


def place_ends(array, own_key, smallest, high):
    longest = array.shape.index(max(array.shape))
    spots = []
    for shift in (0, 1):
        where = [jax.random.randint(jax.random.fold_in(own_key, axis), (), 0, length) for axis, length in enumerate(array.shape)]
        where[longest] = (where[longest] + shift) % array.shape[longest]
        spots.append(tuple(where))
    return array.at[spots[0]].set(smallest).at[spots[1]].set(high)


def block_scale(key, extent, split, smallest, top_value):
    level = 1.0
    for axis_at, shards_of in split:
        heights = jax.random.uniform(jax.random.fold_in(jax.random.fold_in(key, 6), axis_at), (shards_of,), jnp.float32, smallest / len(split), top_value / len(split))
        level = level * jnp.repeat(jnp.exp(heights), extent[axis_at] // shards_of).reshape((-1,) + (1,) * (len(extent) - 1 - axis_at))
    return level


def gaussian(own_key, shape, spread, reach, pieces=(), kind=jnp.bfloat16):
    entries = jax.random.normal(own_key, shape, jnp.float32) * spread
    if len(pieces) > 0:
        entries = block_scale(own_key, shape, pieces, -0.22, 0.18) * entries
    return jnp.clip(entries, min=-reach, max=reach).astype(kind)


def setup_inputs(seed: int = 0) -> dict:
    keys = jax.random.split(jax.random.key(seed), 6)
    activations = gaussian(keys[0], (SEQS, LEN, D), 1.0, 6.0, ((0, 8), (2, 4)))
    out_grads = gaussian(keys[1], (SEQS, LEN, D), 1.0, 6.0, ((0, 8), (2, 4)))
    lengths = place_ends(jax.random.randint(keys[2], (SEQS,), 1, LEN + 1), jax.random.fold_in(keys[2], 1), 1, LEN).astype(jnp.int32)
    proj_in = gaussian(keys[3], (R_IN, D), D ** -0.5, 0.09375, ((1, 4),))
    proj_out = gaussian(keys[4], (R_OUT, D), D ** -0.5, 0.09375, ((1, 4),))
    return {"activations": activations, "out_grads": out_grads, "lengths": lengths, "proj_in": proj_in, "proj_out": proj_out}


def reference(activations, out_grads, lengths, proj_in, proj_out):
    positions = jnp.arange(LEN, dtype=jnp.int32)
    token_mask = (positions[None, :] < lengths[:, None]).astype(jnp.float32)

    def sketch_one(inputs):
        act_rows, grad_rows, mask_row = inputs
        left_proj = jnp.dot(grad_rows, proj_out.T, preferred_element_type=jnp.float32) * mask_row[:, None]
        right_proj = jnp.dot(act_rows, proj_in.T, preferred_element_type=jnp.float32)
        outer = jnp.dot(left_proj.T, right_proj, precision=lax.Precision.HIGHEST, preferred_element_type=jnp.float32)
        return (outer * (1.0 / math.sqrt(LEN))).reshape(-1).astype(jnp.bfloat16)
    sketches = lax.map(sketch_one, (activations, out_grads, token_mask))
    kernel = jnp.dot(sketches, sketches.T, preferred_element_type=jnp.float32)
    return kernel * (1.0 / (R_OUT * R_IN))
```

```python
import functools
import math

import jax
import jax.numpy as jnp
from jax import lax
from jax.experimental import pallas as pl
from jax.experimental.pallas import tpu as pltpu
from jax.sharding import PartitionSpec as P

CORES = 2
GROUP = 4
F32 = jnp.float32
BF16 = jnp.bfloat16
NT = (((1,), (1,)), ((), ()))
TN = (((0,), (0,)), ((), ()))


def fused_kernel(
    n_shard, n_example, chunks, seq_len, scale_sketch, scale_kernel,
    len_ref, acts_ref, grads_ref, pin_ref, pout_ref, out_ref,
    wide, g_buf, a_buf, own1, send1, recv1, sk, arr, tall, gath, ksend, krecv,
    in_sem, s1s, s1r, a2s, a2r, zs, zr, bs, br, kss, krs,
):
    S, G, C, T = n_shard, GROUP, chunks, seq_len
    Z = n_example // CORES
    H = G // 2
    rows_out = pout_ref.shape[0]
    per = rows_out // S
    lanes = pin_ref.shape[0]
    block = S * G
    rows_dev = C * block
    me = lax.axis_index("shard")
    ex = lax.axis_index("example")
    z, core = ex // CORES, ex % CORES
    sib = z * CORES + (1 - core)

    def shard_at(k):
        return lax.rem(me + k, S)

    def z_to(k):
        return lax.rem(z + k, Z) * CORES + core

    def z_from(k):
        return lax.rem(z + Z - k, Z)

    def remote(src, dst, ss, rs, shard, example):
        return pltpu.make_async_remote_copy(
            src_ref=src, dst_ref=dst, send_sem=ss, recv_sem=rs,
            device_id=(shard, example), device_id_type=pl.DeviceIdType.MESH,
        )

    def copy1(c, k):
        return remote(send1.at[c, k - 1], recv1.at[c, k - 1], s1s.at[c, k - 1], s1r.at[c, k - 1], shard_at(k), ex)

    def copy2(c, k):
        return remote(sk.at[c, shard_at(k)], arr.at[c, me], a2s.at[c, k - 1], a2r.at[c, k - 1], shard_at(k), ex)

    def rows_of(e, c):
        return pl.ds(pl.multiple_of(e * rows_dev + c * block, 16), block)

    def copyz(c, k):
        here = gath.at[rows_of(ex, c), :]
        return remote(here, here, zs.at[c, k - 1], zr.at[c, k - 1], me, z_to(k))

    def copyb(c, k):
        here = gath.at[rows_of(z_from(k) * CORES + core, c), :]
        return remote(here, here, bs.at[c, k], br.at[c, k], me, sib)

    def copyk(k):
        return remote(ksend.at[k - 1], krecv.at[k - 1], kss.at[k - 1], krs.at[k - 1], shard_at(k), ex)

    def reads(u, slot):
        c, k = u // S, lax.rem(u, S) + 1
        row = pl.multiple_of((c * block + shard_at(k) * G) * T, 128)
        return (
            pltpu.make_async_copy(grads_ref.at[pl.ds(row, G * T), :], g_buf.at[slot], in_sem.at[slot, 0]),
            pltpu.make_async_copy(acts_ref.at[pl.ds(row, G * T), :], a_buf.at[slot], in_sem.at[slot, 1]),
        )

    for r in reads(0, 0):
        r.start()
    for r in reads(1, 1):
        r.start()

    barrier = pltpu.get_barrier_semaphore()
    for k in range(1, S):
        pl.semaphore_signal(barrier, inc=1, device_id=(shard_at(k), ex), device_id_type=pl.DeviceIdType.MESH)
    for k in range(1, Z):
        pl.semaphore_signal(barrier, inc=1, device_id=(me, z_to(k)), device_id_type=pl.DeviceIdType.MESH)
    pl.semaphore_signal(barrier, inc=1, device_id=(me, sib), device_id_type=pl.DeviceIdType.MESH)

    wide[...] = jnp.zeros_like(wide)
    wide[0, 0:rows_out, :] = pout_ref[...]
    wide[1, rows_out : 2 * rows_out, :] = pout_ref[...]
    pl.semaphore_wait(barrier, S + Z - 1)

    def project(slot, put):
        left = lax.dot_general(g_buf[slot, 0 : H * T, :], wide[0], NT, preferred_element_type=F32)
        left += lax.dot_general(g_buf[slot, H * T :, :], wide[1], NT, preferred_element_type=F32)
        right = lax.dot_general(a_buf[slot], pin_ref[...], NT, preferred_element_type=F32)
        put(0, H * T, left)
        put(H * T, (H + G) * T, right)

    def chunk_body(c, carry):
        for kk in range(S):
            u = c * S + kk
            slot = kk % 2
            for r in reads(u, slot):
                r.wait()
            k = kk + 1
            if k < S:
                def put(lo, hi, v, k=k):
                    send1[c, k - 1, lo:hi, :] = v.astype(BF16)
                project(slot, put)
                copy1(c, k).start()
            else:
                def put(lo, hi, v):
                    own1[c, lo:hi, :] = v
                project(slot, put)

            @pl.when(u + 2 < C * S)
            def _():
                for r in reads(u + 2, slot):
                    r.start()
        return carry

    lax.fori_loop(0, C, chunk_body, 0)

    def make_sketch(c):
        for k in range(1, S):
            copy1(c, k).wait_recv()
        token = lax.broadcasted_iota(jnp.int32, (T, lanes), 0)

        def whole(i):
            at = slice(i * T, (i + 1) * T)
            v = own1[c, at, :]
            for k in range(1, S):
                v = v + recv1[c, k - 1, at, :].astype(F32)
            return v

        first = c * block + me * G
        for p in range(H):
            left = whole(p)
            for half in range(2):
                n = p + half * H
                right = whole(H + n)
                right = jnp.where(token < len_ref[first + n], right, 0.0)
                both = lax.dot_general(left, right, TN, precision=lax.Precision.HIGHEST, preferred_element_type=F32)
                mine = (both[half * rows_out : (half + 1) * rows_out, :] * scale_sketch).astype(BF16)
                for j in range(S):
                    sk[c, j, n] = mine[j * per : (j + 1) * per, :]
        for k in range(1, S):
            copy2(c, k).start()
        arr[c, me] = sk[c, me]

    def spread(c):
        for k in range(1, S):
            copy2(c, k).wait_recv()
        tall[...] = arr[c].reshape(block * per, lanes).astype(F32)
        at = rows_of(ex, c)
        for o in range(per):
            gath[at, o * lanes : (o + 1) * lanes] = tall[pl.ds(o, block, stride=per), :].astype(BF16)
        for k in range(1, Z):
            copyz(c, k).start()
        copyb(c, 0).start()

    def pass_on(c):
        for k in range(1, Z):
            copyz(c, k).wait_recv()
            copyb(c, k).start()

    LAG2, LAG3 = 1, 2

    def tail_body(i, carry):
        @pl.when(i < C)
        def _():
            make_sketch(i)

        @pl.when((i >= LAG2) & (i < C + LAG2))
        def _():
            spread(i - LAG2)

        @pl.when(i >= LAG3)
        def _():
            pass_on(i - LAG3)
        return carry

    lax.fori_loop(0, C + LAG3, tail_body, 0)

    def gather_wait(c, carry):
        for k in range(Z):
            copyb(c, k).wait_recv()
        return carry

    lax.fori_loop(0, C, gather_wait, 0)

    cols = gath.shape[0] // S
    mine = gath.at[pl.ds(pl.multiple_of(ex * rows_dev, 16), rows_dev), :]

    def tile(j):
        other = gath[pl.ds(pl.multiple_of(j * cols, 16), cols), :]
        return lax.dot_general(mine[...], other, NT, preferred_element_type=F32)

    for k in range(1, S):
        ksend[k - 1] = tile(shard_at(k))
        copyk(k).start()
    total = tile(me)

    def drain(c, carry):
        for k in range(1, S):
            copy1(c, k).wait_send()
            copy2(c, k).wait_send()
        for k in range(1, Z):
            copyz(c, k).wait_send()
        for k in range(Z):
            copyb(c, k).wait_send()
        return carry

    lax.fori_loop(0, C, drain, 0)
    for k in range(1, S):
        copyk(k).wait()
        total = total + krecv[k - 1]
    out_ref[...] = total * scale_kernel


def fused(activations, out_grads, lengths, proj_in, proj_out):
    S, E = lax.axis_size("shard"), lax.axis_size("example")
    rows, T, depth = activations.shape
    rows_out, cols_in = proj_out.shape[0], proj_in.shape[0]
    per = rows_out // S
    G, C, Z = GROUP, rows // (S * GROUP), E // CORES
    unit = (G + G // 2) * T
    kernel = functools.partial(
        fused_kernel, S, E, C, T, 1.0 / math.sqrt(T), 1.0 / (rows_out * cols_in)
    )
    dma = pltpu.SemaphoreType.DMA
    cols = rows * E // S
    macs = rows * T * depth * (rows_out + cols_in) + rows * rows * E * per * cols_in
    return pl.pallas_call(
        kernel,
        out_shape=jax.ShapeDtypeStruct((rows, cols), F32),
        in_specs=[
            pl.BlockSpec(memory_space=pltpu.SMEM),
            pl.BlockSpec(memory_space=pl.ANY),
            pl.BlockSpec(memory_space=pl.ANY),
            pl.BlockSpec(memory_space=pltpu.VMEM),
            pl.BlockSpec(memory_space=pltpu.VMEM),
        ],
        out_specs=pl.BlockSpec(memory_space=pltpu.VMEM),
        scratch_shapes=[
            pltpu.VMEM((2, 2 * rows_out, depth), BF16),
            pltpu.VMEM((2, G * T, depth), BF16),
            pltpu.VMEM((2, G * T, depth), BF16),
            pltpu.VMEM((C, unit, cols_in), F32),
            pltpu.VMEM((C, S - 1, unit, cols_in), BF16),
            pltpu.VMEM((C, S - 1, unit, cols_in), BF16),
            pltpu.VMEM((C, S, G, per, cols_in), BF16),
            pltpu.VMEM((C, S, G, per, cols_in), BF16),
            pltpu.VMEM((S * G * per, cols_in), F32),
            pltpu.VMEM((E * rows, per * cols_in), BF16),
            pltpu.VMEM((S - 1, rows, cols), F32),
            pltpu.VMEM((S - 1, rows, cols), F32),
            dma((2, 2)),
            dma((C, S - 1)),
            dma((C, S - 1)),
            dma((C, S - 1)),
            dma((C, S - 1)),
            dma((C, Z - 1)),
            dma((C, Z - 1)),
            dma((C, Z)),
            dma((C, Z)),
            dma((S - 1,)),
            dma((S - 1,)),
        ],
        compiler_params=pltpu.CompilerParams(
            collective_id=0, has_side_effects=True, vmem_limit_bytes=48 * 2**20
        ),
        cost_estimate=pl.CostEstimate(
            flops=2 * macs, bytes_accessed=4 * rows * T * depth, transcendentals=0
        ),
    )(
        lengths,
        activations.reshape(rows * T, depth),
        out_grads.reshape(rows * T, depth),
        proj_in,
        proj_out,
    )


def plain(activations, out_grads, lengths, proj_in, proj_out):
    n_shard = lax.axis_size("shard")
    rows, seq_len = activations.shape[:2]
    rows_out, cols_in = proj_out.shape[0], proj_in.shape[0]
    per_shard = rows_out // n_shard
    positions = lax.broadcasted_iota(jnp.int32, (rows, seq_len), 1)
    token_mask = (positions < lengths[:, None]).astype(F32)
    left = jnp.einsum("btd,od->bto", out_grads, proj_out, preferred_element_type=F32)
    left = left * token_mask[:, :, None]
    right = jnp.einsum("btd,id->bti", activations, proj_in, preferred_element_type=F32)
    left = lax.psum_scatter(left, "shard", scatter_dimension=0, tiled=True)
    right = lax.psum_scatter(right, "shard", scatter_dimension=0, tiled=True)
    sketch = jnp.einsum(
        "bto,bti->boi", left, right, precision=lax.Precision.HIGHEST, preferred_element_type=F32
    )
    sketch = (sketch * (1.0 / math.sqrt(seq_len))).astype(BF16)
    sketch = lax.all_to_all(sketch, "shard", split_axis=1, concat_axis=0, tiled=True)
    sketch = sketch.reshape(rows, per_shard * cols_in)
    every = lax.all_gather(sketch, "example", axis=0, tiled=True)
    tiles = jnp.einsum("ad,bd->ab", sketch, every, preferred_element_type=F32)
    tiles = lax.psum_scatter(tiles, "shard", scatter_dimension=1, tiled=True)
    return tiles * (1.0 / (rows_out * cols_in))


def local(activations, out_grads, lengths, proj_in, proj_out):
    S, E = lax.axis_size("shard"), lax.axis_size("example")
    rows, T, depth = activations.shape
    rows_out, cols_in = proj_out.shape[0], proj_in.shape[0]
    fits = (
        S >= 2 and S % 2 == 0 and E % CORES == 0 and E > CORES
        and rows_out % (16 * S) == 0 and 2 * rows_out == cols_in and cols_in % 128 == 0
        and T % 128 == 0 and depth % 128 == 0
        and rows % (S * GROUP) == 0 and (S * GROUP) % 16 == 0 and (rows * E) % (16 * S) == 0
    )
    return (fused if fits else plain)(activations, out_grads, lengths, proj_in, proj_out)


def solution(mesh):
    return jax.shard_map(
        local,
        mesh=mesh,
        in_specs=(
            P("example", None, "shard"),
            P("example", None, "shard"),
            P("example"),
            P(None, "shard"),
            P(None, "shard"),
        ),
        out_specs=P("example", "shard"),
        check_vma=False,
    )
```

```python
import functools
import math

import jax
import jax.numpy as jnp
from jax import lax
from jax.experimental import pallas as pl
from jax.experimental.pallas import tpu as pltpu
from jax.sharding import PartitionSpec as P

CORES = 2
DEPTH = 4
GROUP = 4
F32 = jnp.float32
BF16 = jnp.bfloat16
NN = (((1,), (0,)), ((), ()))
NT = (((1,), (1,)), ((), ()))
TN = (((0,), (0,)), ((), ()))


def fused_kernel(
    n_shard, n_example, chunks, seq_len, scale_sketch, scale_kernel,
    len_ref, acts_ref, grads_ref, pin_ref, pout_ref, out_ref,
    pin_v, pout_v, wide, right_w, g_buf, a_buf, own1, send1, recv1, sk, arr, tall, gath, ksend, krecv,
    w_sem, in_sem, s1s, s1r, a2s, a2r, zs, zr, bs, br, kss, krs,
):
    S, G, C, T = n_shard, GROUP, chunks, seq_len
    Z = n_example // CORES
    H = G // 2
    rows_out = pout_ref.shape[0]
    per = rows_out // S
    lanes = pin_ref.shape[0]
    block = S * G
    rows_dev = C * block
    me = lax.axis_index("shard")
    ex = lax.axis_index("example")
    z, core = ex // CORES, ex % CORES
    sib = z * CORES + (1 - core)

    def shard_at(k):
        return lax.rem(me + k, S)

    def z_to(k):
        return lax.rem(z + k, Z) * CORES + core

    def z_from(k):
        return lax.rem(z + Z - k, Z)

    def remote(src, dst, ss, rs, shard, example):
        return pltpu.make_async_remote_copy(
            src_ref=src, dst_ref=dst, send_sem=ss, recv_sem=rs,
            device_id=(shard, example), device_id_type=pl.DeviceIdType.MESH,
        )

    def copy1(c, k):
        return remote(send1.at[c, k - 1], recv1.at[c, k - 1], s1s.at[c, k - 1], s1r.at[c, k - 1], shard_at(k), ex)

    def copy2(c, k):
        return remote(sk.at[c, shard_at(k)], arr.at[c, me], a2s.at[c, k - 1], a2r.at[c, k - 1], shard_at(k), ex)

    def rows_of(e, c):
        return pl.ds(pl.multiple_of(e * rows_dev + c * block, 16), block)

    def copyz(c, k):
        here = gath.at[rows_of(ex, c), :]
        return remote(here, here, zs.at[c, k - 1], zr.at[c, k - 1], me, z_to(k))

    def copyb(c, k):
        here = gath.at[rows_of(z_from(k) * CORES + core, c), :]
        return remote(here, here, bs.at[c, k], br.at[c, k], me, sib)

    def copyk(k):
        return remote(ksend.at[k - 1], krecv.at[k - 1], kss.at[k - 1], krs.at[k - 1], shard_at(k), ex)

    def reads(u, slot):
        c, k = u // S, lax.rem(u, S) + 1
        row = pl.multiple_of((c * block + shard_at(k) * G) * T, 128)
        return (
            pltpu.make_async_copy(grads_ref.at[pl.ds(row, G * T), :], g_buf.at[slot], in_sem.at[slot, 0]),
            pltpu.make_async_copy(acts_ref.at[pl.ds(row, G * T), :], a_buf.at[slot], in_sem.at[slot, 1]),
        )

    weights = (
        pltpu.make_async_copy(pin_ref, pin_v, w_sem.at[0]),
        pltpu.make_async_copy(pout_ref, pout_v, w_sem.at[1]),
    )
    for w in weights:
        w.start()
    for u in range(DEPTH):
        for r in reads(u, u):
            r.start()

    barrier = pltpu.get_barrier_semaphore()
    for k in range(1, S):
        pl.semaphore_signal(barrier, inc=1, device_id=(shard_at(k), ex), device_id_type=pl.DeviceIdType.MESH)
    for k in range(1, Z):
        pl.semaphore_signal(barrier, inc=1, device_id=(me, z_to(k)), device_id_type=pl.DeviceIdType.MESH)
    pl.semaphore_signal(barrier, inc=1, device_id=(me, sib), device_id_type=pl.DeviceIdType.MESH)

    for w in weights:
        w.wait()
    right_w[...] = pin_v[...].astype(F32).T.astype(BF16)
    thin = pout_v[...].astype(F32)
    zero = jnp.zeros_like(thin)
    wide[0] = jnp.concatenate([thin, zero], axis=0).T.astype(BF16)
    wide[1] = jnp.concatenate([zero, thin], axis=0).T.astype(BF16)
    pl.semaphore_wait(barrier, S + Z - 1)

    def project(slot, put):
        left = lax.dot_general(g_buf[slot, 0 : H * T, :], wide[0], NN, preferred_element_type=F32)
        left += lax.dot_general(g_buf[slot, H * T :, :], wide[1], NN, preferred_element_type=F32)
        right = lax.dot_general(a_buf[slot], right_w[...], NN, preferred_element_type=F32)
        put(0, H * T, left)
        put(H * T, (H + G) * T, right)

    def project_chunk(c):
        for kk in range(S):
            u = c * S + kk
            slot = kk % DEPTH
            for r in reads(u, slot):
                r.wait()
            k = kk + 1
            if k < S:
                def put(lo, hi, v, k=k):
                    send1[c, k - 1, lo:hi, :] = v.astype(BF16)
                project(slot, put)
                copy1(c, k).start()
            else:
                def put(lo, hi, v):
                    own1[c, lo:hi, :] = v
                project(slot, put)

            @pl.when(u + DEPTH < C * S)
            def _():
                for r in reads(u + DEPTH, slot):
                    r.start()

    def make_sketch(c):
        for k in range(1, S):
            copy1(c, k).wait_recv()
        token = lax.broadcasted_iota(jnp.int32, (T, lanes), 0)

        def whole(i):
            at = slice(i * T, (i + 1) * T)
            v = own1[c, at, :]
            for k in range(1, S):
                v = v + recv1[c, k - 1, at, :].astype(F32)
            return v

        first = c * block + me * G
        for p in range(H):
            left = whole(p)
            for half in range(2):
                n = p + half * H
                right = whole(H + n)
                right = jnp.where(token < len_ref[first + n], right, 0.0)
                both = lax.dot_general(left, right, TN, precision=lax.Precision.HIGHEST, preferred_element_type=F32)
                mine = (both[half * rows_out : (half + 1) * rows_out, :] * scale_sketch).astype(BF16)
                for j in range(S):
                    sk[c, j, n] = mine[j * per : (j + 1) * per, :]
        for k in range(1, S):
            copy2(c, k).start()
        arr[c, me] = sk[c, me]

    def spread(c):
        for k in range(1, S):
            copy2(c, k).wait_recv()
        tall[...] = arr[c].reshape(block * per, lanes).astype(F32)
        at = rows_of(ex, c)
        for o in range(per):
            gath[at, o * lanes : (o + 1) * lanes] = tall[pl.ds(o, block, stride=per), :].astype(BF16)
        for k in range(1, Z):
            copyz(c, k).start()
        copyb(c, 0).start()

    def pass_on(c):
        for k in range(1, Z):
            copyz(c, k).wait_recv()
            copyb(c, k).start()

    steps = (project_chunk, make_sketch, spread, pass_on)

    def body(i, carry):
        for lag, step in enumerate(steps):
            @pl.when((i >= lag) & (i < C + lag))
            def _(lag=lag, step=step):
                step(i - lag)
        return carry

    lax.fori_loop(0, C + len(steps) - 1, body, 0)

    def gather_wait(c, carry):
        for k in range(Z):
            copyb(c, k).wait_recv()
        return carry

    lax.fori_loop(0, C, gather_wait, 0)

    cols = gath.shape[0] // S
    mine = gath.at[pl.ds(pl.multiple_of(ex * rows_dev, 16), rows_dev), :]

    def tile(j):
        other = gath[pl.ds(pl.multiple_of(j * cols, 16), cols), :]
        return lax.dot_general(mine[...], other, NT, preferred_element_type=F32)

    for k in range(1, S):
        ksend[k - 1] = tile(shard_at(k))
        copyk(k).start()
    total = tile(me)

    def drain(c, carry):
        for k in range(1, S):
            copy1(c, k).wait_send()
            copy2(c, k).wait_send()
        for k in range(1, Z):
            copyz(c, k).wait_send()
        for k in range(Z):
            copyb(c, k).wait_send()
        return carry

    lax.fori_loop(0, C, drain, 0)
    for k in range(1, S):
        copyk(k).wait()
        total = total + krecv[k - 1]
    out_ref[...] = total * scale_kernel


def fused(activations, out_grads, lengths, proj_in, proj_out):
    S, E = lax.axis_size("shard"), lax.axis_size("example")
    rows, T, depth = activations.shape
    rows_out, cols_in = proj_out.shape[0], proj_in.shape[0]
    per = rows_out // S
    G, C, Z = GROUP, rows // (S * GROUP), E // CORES
    unit = (G + G // 2) * T
    kernel = functools.partial(
        fused_kernel, S, E, C, T, 1.0 / math.sqrt(T), 1.0 / (rows_out * cols_in)
    )
    dma = pltpu.SemaphoreType.DMA
    cols = rows * E // S
    macs = rows * T * depth * (rows_out + cols_in) + rows * rows * E * per * cols_in
    return pl.pallas_call(
        kernel,
        out_shape=jax.ShapeDtypeStruct((rows, cols), F32),
        in_specs=[
            pl.BlockSpec(memory_space=pltpu.SMEM),
            pl.BlockSpec(memory_space=pl.ANY),
            pl.BlockSpec(memory_space=pl.ANY),
            pl.BlockSpec(memory_space=pl.ANY),
            pl.BlockSpec(memory_space=pl.ANY),
        ],
        out_specs=pl.BlockSpec(memory_space=pltpu.VMEM),
        scratch_shapes=[
            pltpu.VMEM((cols_in, depth), BF16),
            pltpu.VMEM((rows_out, depth), BF16),
            pltpu.VMEM((2, depth, 2 * rows_out), BF16),
            pltpu.VMEM((depth, cols_in), BF16),
            pltpu.VMEM((DEPTH, G * T, depth), BF16),
            pltpu.VMEM((DEPTH, G * T, depth), BF16),
            pltpu.VMEM((C, unit, cols_in), F32),
            pltpu.VMEM((C, S - 1, unit, cols_in), BF16),
            pltpu.VMEM((C, S - 1, unit, cols_in), BF16),
            pltpu.VMEM((C, S, G, per, cols_in), BF16),
            pltpu.VMEM((C, S, G, per, cols_in), BF16),
            pltpu.VMEM((S * G * per, cols_in), F32),
            pltpu.VMEM((E * rows, per * cols_in), BF16),
            pltpu.VMEM((S - 1, rows, cols), F32),
            pltpu.VMEM((S - 1, rows, cols), F32),
            dma((2,)),
            dma((DEPTH, 2)),
            dma((C, S - 1)),
            dma((C, S - 1)),
            dma((C, S - 1)),
            dma((C, S - 1)),
            dma((C, Z - 1)),
            dma((C, Z - 1)),
            dma((C, Z)),
            dma((C, Z)),
            dma((S - 1,)),
            dma((S - 1,)),
        ],
        compiler_params=pltpu.CompilerParams(
            collective_id=0, has_side_effects=True, vmem_limit_bytes=48 * 2**20
        ),
        cost_estimate=pl.CostEstimate(
            flops=2 * macs, bytes_accessed=4 * rows * T * depth, transcendentals=0
        ),
    )(
        lengths,
        activations.reshape(rows * T, depth),
        out_grads.reshape(rows * T, depth),
        proj_in,
        proj_out,
    )


def plain(activations, out_grads, lengths, proj_in, proj_out):
    n_shard = lax.axis_size("shard")
    rows, seq_len = activations.shape[:2]
    rows_out, cols_in = proj_out.shape[0], proj_in.shape[0]
    per_shard = rows_out // n_shard
    positions = lax.broadcasted_iota(jnp.int32, (rows, seq_len), 1)
    token_mask = (positions < lengths[:, None]).astype(F32)
    left = jnp.einsum("btd,od->bto", out_grads, proj_out, preferred_element_type=F32)
    left = left * token_mask[:, :, None]
    right = jnp.einsum("btd,id->bti", activations, proj_in, preferred_element_type=F32)
    left = lax.psum_scatter(left, "shard", scatter_dimension=0, tiled=True)
    right = lax.psum_scatter(right, "shard", scatter_dimension=0, tiled=True)
    sketch = jnp.einsum(
        "bto,bti->boi", left, right, precision=lax.Precision.HIGHEST, preferred_element_type=F32
    )
    sketch = (sketch * (1.0 / math.sqrt(seq_len))).astype(BF16)
    sketch = lax.all_to_all(sketch, "shard", split_axis=1, concat_axis=0, tiled=True)
    sketch = sketch.reshape(rows, per_shard * cols_in)
    every = lax.all_gather(sketch, "example", axis=0, tiled=True)
    tiles = jnp.einsum("ad,bd->ab", sketch, every, preferred_element_type=F32)
    tiles = lax.psum_scatter(tiles, "shard", scatter_dimension=1, tiled=True)
    return tiles * (1.0 / (rows_out * cols_in))


def local(activations, out_grads, lengths, proj_in, proj_out):
    S, E = lax.axis_size("shard"), lax.axis_size("example")
    rows, T, depth = activations.shape
    rows_out, cols_in = proj_out.shape[0], proj_in.shape[0]
    fits = (
        S >= 2 and S % 2 == 0 and E % CORES == 0 and E > CORES
        and rows_out % (16 * S) == 0 and 2 * rows_out == cols_in and cols_in % 128 == 0
        and T % 128 == 0 and depth % 128 == 0
        and rows % (S * GROUP) == 0 and (S * GROUP) % 16 == 0 and (rows * E) % (16 * S) == 0
    )
    return (fused if fits else plain)(activations, out_grads, lengths, proj_in, proj_out)


def solution(mesh):
    return jax.shard_map(
        local,
        mesh=mesh,
        in_specs=(
            P("example", None, "shard"),
            P("example", None, "shard"),
            P("example"),
            P(None, "shard"),
            P(None, "shard"),
        ),
        out_specs=P("example", "shard"),
        check_vma=False,
    )
```
